32 devices in a mesh: expert: 8 (over y, x, core), replica: 4 (over z).
Axes of the slice: x: 2, y: 2, z: 4, core: 2. Of those that a mesh axis runs over, the one named last changes fastest.
Arguments:
- x_rows: bfloat16 [4096, 2048], P(('expert', 'replica')), may hold values from -6 to 6
- out_grad: bfloat16 [4096, 2048], P(('expert', 'replica')), may hold values from -6 to 6
- gate_weight: bfloat16 [16, 2048, 768], P('expert', 'replica'), may hold values from -0.125 to 0.125
- up_weight: bfloat16 [16, 2048, 768], P('expert', 'replica'), may hold values from -0.125 to 0.125
- down_weight: bfloat16 [16, 2048, 768], P('expert', 'replica'), may hold values from -0.21875 to 0.21875
- expert_ids: int32 [4096], P(('expert', 'replica')), may hold values from 0 to 15, as said below
- slot_expert: int32 [8, 4], replicated, may hold values from 0 to 15, as said below
Outputs:
- x_grad: bfloat16 [4096, 2048], P(('expert', 'replica'))
- gate_wgrad: bfloat16 [16, 2048, 768], P('expert', 'replica')
- up_wgrad: bfloat16 [16, 2048, 768], P('expert', 'replica')
- down_wgrad: bfloat16 [16, 2048, 768], P('expert', 'replica')
The draws below stay inside these ranges and needn't reach their ends.
Inputs may be any that keep to these rules, and one draw needn't show every extreme that they name: `expert_ids`: each device's 128 rows name each expert at most 16 times. In every draw, one expert that a single device serves is named exactly 16 times by every device, and so is the other expert of its index. `slot_expert`: row j holds only 2 * j and 2 * j + 1, each of the two at least once.
All inputs are finite; a program needn't handle non-finite values.
Results may differ from the reference program's by a relative error of at most 0.0065.
Values may be sent and summed in bfloat16 or wider, within the bound.
A program may use at most 128 MiB of HBM per device.

```python
import jax
import jax.numpy as jnp
from jax import lax

D = 2048
FF = 768
EXP_DEV = 2
ROWS_DEV = 128
EXPERTS = 16
MOST = 16
SLOTS = 512
TOTAL_ROWS = 4096
N_EXPERT = 8
N_REPLICA = 4


def shared_layout(key):
    count_key, hot_key, order_key = jax.random.split(jax.random.fold_in(key, 5), 3)
    first_servers = jax.random.randint(count_key, (N_EXPERT,), 1, N_REPLICA)
    hottest = jax.random.randint(hot_key, (), 0, N_EXPERT)
    positions = jnp.arange(N_EXPERT, dtype=jnp.int32)
    first_servers = jnp.where(positions == hottest, 1, first_servers)
    orders = jax.vmap(lambda part_key: jax.random.permutation(part_key, N_REPLICA))(jax.random.split(order_key, N_EXPERT))
    places = jnp.argsort(orders, axis=1)
    served = EXP_DEV * positions[:, None] + (places >= first_servers[:, None]).astype(jnp.int32)
    return (hottest.astype(jnp.int32), served.astype(jnp.int32))


def draw_slot_expert(key, part):
    hottest, served = shared_layout(key)
    return served


def draw_expert_ids(key, part):
    hottest, served = shared_layout(key)
    key = jax.random.fold_in(key, 9)
    devices = N_EXPERT * N_REPLICA
    others = (EXPERTS - 2) * MOST
    candidates = jnp.arange(others, dtype=jnp.int32) // MOST
    candidates = jnp.where(candidates < 2 * hottest, candidates, candidates + 2)
    hot_rows = 2 * hottest + jnp.arange(2 * MOST, dtype=jnp.int32) // MOST

    def one_device(device_key):
        pick_key, shuffle_key = jax.random.split(device_key)
        picked = candidates[jax.random.permutation(pick_key, others)[:ROWS_DEV - 2 * MOST]]
        row_experts = jnp.concatenate([hot_rows, picked])
        return row_experts[jax.random.permutation(shuffle_key, ROWS_DEV)]
    return jax.vmap(one_device)(jax.random.split(key, devices)).reshape(TOTAL_ROWS).astype(jnp.int32)


def block_levels(key, extent, cuts, least, largest):
    factor_of, own = 1.0, jax.random.fold_in(key, 6)
    for dim, parts in cuts:
        draws = jnp.exp(jax.random.uniform(jax.random.fold_in(own, dim), (parts,), jnp.float32, least / len(cuts), largest / len(cuts)))
        factor_of = factor_of * jnp.repeat(draws, extent[dim] // parts).reshape([-1 if axis == dim else 1 for axis in range(len(extent))])
    return factor_of


def noise(stream_key, dims, deviation, reach, cuts=(), held_as=jnp.bfloat16):
    level = block_levels(stream_key, dims, cuts, -0.22, 0.18) if cuts else 1.0
    values = jax.random.normal(stream_key, dims, jnp.float32) * deviation * level
    return jnp.minimum(jnp.maximum(values, -reach), reach).astype(held_as)


def setup_inputs(seed: int = 0) -> dict:
    key_of = jax.random.split(jax.random.key(seed), 8)
    return {
        "x_rows": noise(key_of[0], (TOTAL_ROWS, D), 1.0, 6.0, ((0, 32),)),
        "out_grad": noise(key_of[1], (TOTAL_ROWS, D), 1.0, 6.0, ((0, 32),)),
        "gate_weight": noise(key_of[2], (EXPERTS, D, FF), D ** -0.5, 0.125, ((0, 8), (1, 4))),
        "up_weight": noise(key_of[3], (EXPERTS, D, FF), D ** -0.5, 0.125, ((0, 8), (1, 4))),
        "down_weight": noise(key_of[4], (EXPERTS, D, FF), FF ** -0.5, 0.21875, ((0, 8), (1, 4))),
        "expert_ids": draw_expert_ids(jax.random.fold_in(key_of[7], 71), 0),
        "slot_expert": draw_slot_expert(jax.random.fold_in(key_of[7], 71), 0),
    }


def routing(row_experts, slot_expert, replica_here, expert_count):
    matches = slot_expert[None, :, :] == row_experts[:, None, None]
    serve_mask = jnp.sum(matches.astype(jnp.int32), axis=1)
    servers = jnp.sum(serve_mask, axis=1)
    wanted = replica_here % servers + 1
    running = jnp.cumsum(serve_mask, axis=1)
    replica_ids = lax.broadcasted_iota(jnp.int32, serve_mask.shape, 1)
    chosen = (serve_mask == 1) & (running == wanted[:, None])
    target = jnp.sum(jnp.where(chosen, replica_ids, 0), axis=1).astype(jnp.int32)
    expert_range = lax.broadcasted_iota(jnp.int32, (row_experts.shape[0], expert_count), 1)
    one_hot = (expert_range == row_experts[:, None]).astype(jnp.int32)
    before = jnp.cumsum(one_hot, axis=0) - one_hot
    row_rank = jnp.sum(before * one_hot, axis=1).astype(jnp.int32)
    device_dst = (row_experts // EXP_DEV) * slot_expert.shape[1] + target
    return device_dst.astype(jnp.int32), row_rank


def expert_backward(rows_in, rows_grad, gate_matrix, up_matrix, down_matrix):
    gate_pre = jnp.dot(rows_in, gate_matrix, preferred_element_type=jnp.float32)
    up_pre = jnp.dot(rows_in, up_matrix, preferred_element_type=jnp.float32)
    sigmoid_gate = jax.nn.sigmoid(gate_pre)
    silu_gate = gate_pre * sigmoid_gate
    hidden = (silu_gate * up_pre).astype(jnp.bfloat16)
    hidden_grad = jnp.dot(rows_grad, down_matrix, preferred_element_type=jnp.float32)
    up_part = (hidden_grad * silu_gate).astype(jnp.bfloat16)
    gate_part = (hidden_grad * up_pre * sigmoid_gate * (1.0 + gate_pre * (1.0 - sigmoid_gate))).astype(jnp.bfloat16)
    contract_hidden = (((1,), (1,)), ((), ()))
    slot_grad = lax.dot_general(gate_part, gate_matrix, contract_hidden, preferred_element_type=jnp.float32)
    slot_grad = slot_grad + lax.dot_general(up_part, up_matrix, contract_hidden, preferred_element_type=jnp.float32)
    contract_rows = (((0,), (0,)), ((), ()))
    gate_term = lax.dot_general(rows_in, gate_part, contract_rows, preferred_element_type=jnp.float32)
    up_term = lax.dot_general(rows_in, up_part, contract_rows, preferred_element_type=jnp.float32)
    down_term = lax.dot_general(rows_grad, hidden, contract_rows, preferred_element_type=jnp.float32)
    return slot_grad.astype(jnp.bfloat16), gate_term, up_term, down_term


def reference(x_rows, out_grad, gate_weight, up_weight, down_weight, expert_ids, slot_expert):
    devices = N_EXPERT * N_REPLICA
    per_device = expert_ids.reshape(devices, ROWS_DEV)
    replica_here = jnp.arange(devices, dtype=jnp.int32) % N_REPLICA
    device_dst, row_rank = jax.vmap(lambda row_experts, here: routing(row_experts, slot_expert, here, EXPERTS))(per_device, replica_here)
    sender = lax.broadcasted_iota(jnp.int32, (devices, ROWS_DEV), 0)
    recv_slot = (sender * MOST + row_rank).astype(jnp.int32)
    row_index = jnp.arange(TOTAL_ROWS, dtype=jnp.int32)
    table = jnp.full((devices, SLOTS), TOTAL_ROWS, jnp.int32)
    table = table.at[device_dst.reshape(-1), recv_slot.reshape(-1)].set(row_index)
    inputs_pad = jnp.concatenate([x_rows, jnp.zeros((1, D), x_rows.dtype)], axis=0)
    grads_pad = jnp.concatenate([out_grad, jnp.zeros((1, D), out_grad.dtype)], axis=0)

    def one_index(position):
        slot_grads = []
        served_list = []
        gate_terms = []
        up_terms = []
        down_terms = []
        for column in range(N_REPLICA):
            device = position * N_REPLICA + column
            picks = lax.dynamic_index_in_dim(table, device, 0, keepdims=False)
            served = slot_expert[position, column]
            gate_matrix = lax.dynamic_index_in_dim(gate_weight, served, 0, keepdims=False)
            up_matrix = lax.dynamic_index_in_dim(up_weight, served, 0, keepdims=False)
            down_matrix = lax.dynamic_index_in_dim(down_weight, served, 0, keepdims=False)
            slot_grad, gate_term, up_term, down_term = expert_backward(inputs_pad[picks], grads_pad[picks], gate_matrix, up_matrix, down_matrix)
            rounded = lax.optimization_barrier((gate_term.astype(jnp.bfloat16), up_term.astype(jnp.bfloat16), down_term.astype(jnp.bfloat16)))
            slot_grads.append(slot_grad)
            served_list.append(served)
            gate_terms.append(rounded[0])
            up_terms.append(rounded[1])
            down_terms.append(rounded[2])
        gate_out = []
        up_out = []
        down_out = []
        for local in range(EXP_DEV):
            expert = position * EXP_DEV + local
            gate_total = jnp.zeros((D, FF), jnp.float32)
            up_total = jnp.zeros((D, FF), jnp.float32)
            down_total = jnp.zeros((D, FF), jnp.float32)
            server_count = jnp.zeros((), jnp.float32)
            for column in range(N_REPLICA):
                hit = served_list[column] == expert
                server_count = server_count + jnp.where(hit, 1.0, 0.0).astype(jnp.float32)
                gate_total = gate_total + jnp.where(hit, gate_terms[column].astype(jnp.float32), 0.0)
                up_total = up_total + jnp.where(hit, up_terms[column].astype(jnp.float32), 0.0)
                down_total = down_total + jnp.where(hit, down_terms[column].astype(jnp.float32), 0.0)
            gate_out.append((gate_total / server_count).astype(jnp.bfloat16))
            up_out.append((up_total / server_count).astype(jnp.bfloat16))
            down_out.append((down_total / server_count).astype(jnp.bfloat16))
        return jnp.stack(slot_grads), jnp.stack(gate_out), jnp.stack(up_out), jnp.stack(down_out)

    slot_all, gate_all, up_all, down_all = lax.map(one_index, jnp.arange(N_EXPERT, dtype=jnp.int32))
    slot_flat = slot_all.reshape(devices * SLOTS, D)
    x_grad = slot_flat[(device_dst * SLOTS + recv_slot).reshape(-1)]
    gate_wgrad = gate_all.reshape(EXPERTS, D, FF)
    up_wgrad = up_all.reshape(EXPERTS, D, FF)
    down_wgrad = down_all.reshape(EXPERTS, D, FF)
    return x_grad, gate_wgrad, up_wgrad, down_wgrad
```

```python
import jax
import jax.numpy as jnp
from jax import lax
from jax.sharding import PartitionSpec as P

EXP_DEV = 2
BF = jnp.bfloat16
F32 = jnp.float32


def send_slots(row_experts, expert_count, capacity):
    rows = row_experts.shape[0]
    expert_range = lax.broadcasted_iota(jnp.int32, (rows, expert_count), 1)
    one_hot = (expert_range == row_experts[:, None]).astype(BF)
    earlier = lax.broadcasted_iota(jnp.int32, (rows, rows), 1) < lax.broadcasted_iota(
        jnp.int32, (rows, rows), 0
    )
    before = jnp.dot(earlier.astype(BF), one_hot, preferred_element_type=F32)
    rank = jnp.sum(before * one_hot.astype(F32), axis=1)
    return row_experts.astype(F32) * capacity + rank


def middle(rows_in, rows_grad, gate_w, up_w, down_w):
    fwd = (((2,), (1,)), ((0,), (0,)))
    dot = lambda a, b, dims: lax.dot_general(a, b, dims, preferred_element_type=F32)
    partial = jnp.stack(
        [dot(rows_in, gate_w, fwd), dot(rows_in, up_w, fwd), dot(rows_grad, down_w, fwd)]
    ).astype(BF)
    total = lax.psum(partial, "replica").astype(F32)
    gate_pre, up_pre, hidden_grad = total[0], total[1], total[2]
    sig = jax.nn.sigmoid(gate_pre)
    silu = gate_pre * sig
    hidden = (silu * up_pre).astype(BF)
    up_part = (hidden_grad * silu).astype(BF)
    gate_part = (hidden_grad * up_pre * sig * (1.0 + gate_pre * (1.0 - sig))).astype(BF)
    back = (((2,), (2,)), ((0,), (0,)))
    slot_grad = (dot(gate_part, gate_w, back) + dot(up_part, up_w, back)).astype(BF)
    over_rows = (((1,), (1,)), ((0,), (0,)))
    return (
        slot_grad,
        dot(rows_in, gate_part, over_rows),
        dot(rows_in, up_part, over_rows),
        dot(rows_grad, hidden, over_rows),
    )


def on_device(x_rows, out_grad, gate_weight, up_weight, down_weight, expert_ids, slot_expert):
    expert_here = lax.axis_index("expert")
    n_expert = lax.axis_size("expert")
    n_replica = lax.axis_size("replica")
    rows, features = x_rows.shape
    part = features // n_replica
    experts_all = EXP_DEV * n_expert
    capacity = max(2, 2 * rows // experts_all)
    slots = experts_all * capacity
    own_row = lax.dynamic_index_in_dim(slot_expert, expert_here, 0, keepdims=False)
    local_all = own_row - EXP_DEV * expert_here
    servers = jnp.sum(
        (jnp.arange(EXP_DEV, dtype=jnp.int32)[:, None] == local_all[None, :]).astype(F32), axis=1
    )[:, None, None]

    slot_row = send_slots(expert_ids, experts_all, capacity)
    slot_row = jnp.pad(slot_row.astype(BF), (0, part - rows))
    slot_rows = jnp.broadcast_to(slot_row[None, None, :], (n_replica, 16, part))
    split = lambda a: a.reshape(rows, n_replica, part).transpose(1, 0, 2)
    outgoing = jnp.concatenate([split(x_rows), split(out_grad), slot_rows], axis=1)
    arrived = lax.all_to_all(outgoing, "replica", split_axis=0, concat_axis=0, tiled=True)
    slot_of = arrived[:, 2 * rows, :rows].astype(jnp.int32)
    pick = (
        slot_of[:, None, :] == lax.broadcasted_iota(jnp.int32, (n_replica, slots, rows), 1)
    ).astype(BF)
    pairs = arrived[:, : 2 * rows].reshape(n_replica, 2, rows, part)
    packed = jnp.einsum("qsr,qarf->saqf", pick, pairs, preferred_element_type=F32).astype(BF)
    packed = packed.reshape(n_expert, EXP_DEV * capacity, 2, n_replica, part)
    packed = lax.all_to_all(packed, "expert", split_axis=0, concat_axis=0, tiled=True)
    packed = packed.reshape(n_expert, EXP_DEV, capacity, 2, n_replica, part)
    packed = packed.transpose(3, 1, 0, 4, 2, 5).reshape(2, EXP_DEV, -1, part)

    slot_grad, gate_sum, up_sum, down_sum = middle(
        packed[0], packed[1], gate_weight, up_weight, down_weight
    )
    back = slot_grad.reshape(EXP_DEV, n_expert, n_replica, capacity, part).transpose(1, 2, 0, 3, 4)
    back = lax.all_to_all(back, "expert", split_axis=0, concat_axis=0, tiled=True)
    back = back.transpose(1, 0, 2, 3, 4).reshape(n_replica, slots, part)
    x_part = jnp.einsum("qsr,qsf->qrf", pick, back, preferred_element_type=F32).astype(BF)
    x_grad = lax.all_to_all(x_part, "replica", split_axis=0, concat_axis=0, tiled=True)
    x_grad = x_grad.transpose(1, 0, 2).reshape(rows, features)
    mean = lambda total: (total / servers).astype(BF)
    return (x_grad, mean(gate_sum), mean(up_sum), mean(down_sum))


def solution(mesh):
    return jax.shard_map(
        on_device,
        mesh=mesh,
        in_specs=(
            P(("expert", "replica"), None),
            P(("expert", "replica"), None),
            P("expert", "replica", None),
            P("expert", "replica", None),
            P("expert", "replica", None),
            P(("expert", "replica")),
            P(),
        ),
        out_specs=(
            P(("expert", "replica"), None),
            P("expert", "replica", None),
            P("expert", "replica", None),
            P("expert", "replica", None),
        ),
        check_vma=False,
    )
```

```python
import functools

import jax
import jax.numpy as jnp
from jax import lax
from jax.experimental import pallas as pl
from jax.experimental.pallas import tpu as pltpu
from jax.sharding import PartitionSpec as P

EXP_DEV = 2
BF = jnp.bfloat16
F32 = jnp.float32


def send_slots(row_experts, expert_count, capacity):
    rows = row_experts.shape[0]
    expert_range = lax.broadcasted_iota(jnp.int32, (rows, expert_count), 1)
    one_hot = (expert_range == row_experts[:, None]).astype(BF)
    earlier = lax.broadcasted_iota(jnp.int32, (rows, rows), 1) < lax.broadcasted_iota(
        jnp.int32, (rows, rows), 0
    )
    before = jnp.dot(earlier.astype(BF), one_hot, preferred_element_type=F32)
    rank = jnp.sum(before * one_hot.astype(F32), axis=1)
    return row_experts.astype(F32) * capacity + rank


def line_kernel(
    n_replica, x_ref, g_ref, a_ref, b_ref, c_ref, gate_ref, up_ref, hid_ref,
    own, from_left, from_right, to_right, to_left, total, send_r, recv_r, send_l, recv_l,
):
    here = lax.axis_index("replica")
    last = n_replica - 1
    n_chunk, chunk, _ = own.shape
    hidden = a_ref.shape[2]
    rows = x_ref.shape[1]
    block = min(128, rows)
    per_block = block // chunk

    def rightward(c):
        return pltpu.make_async_remote_copy(
            src_ref=to_right.at[c], dst_ref=from_left.at[c],
            send_sem=send_r.at[c], recv_sem=recv_r.at[c],
            device_id={"replica": lax.rem(here + 1, n_replica)},
            device_id_type=pl.DeviceIdType.MESH,
        )

    def leftward(c):
        return pltpu.make_async_remote_copy(
            src_ref=to_left.at[c], dst_ref=from_right.at[c],
            send_sem=send_l.at[c], recv_sem=recv_l.at[c],
            device_id={"replica": lax.rem(here + last, n_replica)},
            device_id_type=pl.DeviceIdType.MESH,
        )

    barrier = pltpu.get_barrier_semaphore()

    @pl.when(here > 0)
    def _():
        pl.semaphore_signal(
            barrier, inc=1, device_id={"replica": lax.rem(here + last, n_replica)},
            device_id_type=pl.DeviceIdType.MESH,
        )

    @pl.when(here < last)
    def _():
        pl.semaphore_signal(
            barrier, inc=1, device_id={"replica": lax.rem(here + 1, n_replica)},
            device_id_type=pl.DeviceIdType.MESH,
        )

    @pl.when((here > 0) & (here < last))
    def _():
        pl.semaphore_wait(barrier, 2)

    @pl.when((here == 0) | (here == last))
    def _():
        pl.semaphore_wait(barrier, 1)

    for e in range(EXP_DEV):

        @pl.loop(0, rows // block)
        def _(b):
            at = pl.ds(pl.multiple_of(b * block, block), block)
            first = e * (rows // chunk) + b * per_block
            for w, (lhs, rhs) in enumerate(((x_ref, a_ref), (x_ref, b_ref), (g_ref, c_ref))):
                part = jnp.dot(lhs[e, at, :], rhs[e], preferred_element_type=F32)
                own[pl.ds(first, per_block), :, w * hidden : (w + 1) * hidden] = part.reshape(
                    per_block, chunk, hidden
                )
            for k in range(per_block):

                @pl.when(here == 0)
                def _():
                    to_right[first + k] = own[first + k].astype(BF)
                    rightward(first + k).start()

                @pl.when(here == last)
                def _():
                    to_left[first + k] = own[first + k].astype(BF)
                    leftward(first + k).start()

    @pl.loop(0, n_chunk + last)
    def _(t):
        c_left = t - here
        c_right = t - (last - here)
        done = t - last

        @pl.when((here > 0) & (c_left >= 0) & (c_left < n_chunk))
        def _():
            rightward(c_left).wait_recv()

            @pl.when(here < last)
            def _():
                to_right[c_left] = (own[c_left] + from_left[c_left].astype(F32)).astype(BF)
                rightward(c_left).start()

        @pl.when((here < last) & (c_right >= 0) & (c_right < n_chunk))
        def _():
            leftward(c_right).wait_recv()

            @pl.when(here > 0)
            def _():
                to_left[c_right] = (own[c_right] + from_right[c_right].astype(F32)).astype(BF)
                leftward(c_right).start()

        @pl.when(done >= 0)
        def _():
            total[...] = own[done]

            @pl.when(here > 0)
            def _():
                total[...] += from_left[done].astype(F32)

            @pl.when(here < last)
            def _():
                total[...] += from_right[done].astype(F32)

            gate_pre = total[:, :hidden]
            up_pre = total[:, hidden : 2 * hidden]
            hidden_grad = total[:, 2 * hidden :]
            sig = jax.nn.sigmoid(gate_pre)
            silu = gate_pre * sig
            hid_ref[done] = (silu * up_pre).astype(BF)
            up_ref[done] = (hidden_grad * silu).astype(BF)
            gate_ref[done] = (
                hidden_grad * up_pre * sig * (1.0 + gate_pre * (1.0 - sig))
            ).astype(BF)

    @pl.loop(0, n_chunk)
    def _(c):
        @pl.when(here < last)
        def _():
            rightward(c).wait_send()

        @pl.when(here > 0)
        def _():
            leftward(c).wait_send()


def hidden_parts(n_replica, rows_in, rows_grad, gate_w, up_w, down_w):
    rows, part = rows_in.shape[1:]
    hidden = gate_w.shape[2]
    chunk = min(32, rows)
    n_chunk = EXP_DEV * rows // chunk
    wide = (n_chunk, chunk, 3 * hidden)
    vmem = pl.BlockSpec(memory_space=pltpu.VMEM)
    outs = pl.pallas_call(
        functools.partial(line_kernel, n_replica),
        out_shape=[jax.ShapeDtypeStruct((n_chunk, chunk, hidden), BF)] * 3,
        in_specs=[vmem] * 5,
        out_specs=[vmem] * 3,
        scratch_shapes=[
            pltpu.VMEM(wide, F32),
            pltpu.VMEM(wide, BF),
            pltpu.VMEM(wide, BF),
            pltpu.VMEM(wide, BF),
            pltpu.VMEM(wide, BF),
            pltpu.VMEM(wide[1:], F32),
            pltpu.SemaphoreType.DMA((n_chunk,)),
            pltpu.SemaphoreType.DMA((n_chunk,)),
            pltpu.SemaphoreType.DMA((n_chunk,)),
            pltpu.SemaphoreType.DMA((n_chunk,)),
        ],
        compiler_params=pltpu.CompilerParams(
            collective_id=0, has_side_effects=True, vmem_limit_bytes=54 * 2**20
        ),
        cost_estimate=pl.CostEstimate(
            flops=6 * EXP_DEV * rows * part * hidden, bytes_accessed=2**24, transcendentals=2**20
        ),
    )(rows_in, rows_grad, gate_w, up_w, down_w)
    return [o.reshape(EXP_DEV, rows, hidden) for o in outs]


def middle(n_replica, rows_in, rows_grad, gate_w, up_w, down_w):
    gate_part, up_part, hidden = hidden_parts(
        n_replica, rows_in, rows_grad, gate_w, up_w, down_w
    )
    dot = lambda a, b, dims: lax.dot_general(a, b, dims, preferred_element_type=F32)
    back = (((2,), (2,)), ((0,), (0,)))
    slot_grad = (dot(gate_part, gate_w, back) + dot(up_part, up_w, back)).astype(BF)
    over_rows = (((1,), (1,)), ((0,), (0,)))
    return (
        slot_grad,
        dot(rows_in, gate_part, over_rows),
        dot(rows_in, up_part, over_rows),
        dot(rows_grad, hidden, over_rows),
    )


def on_device(x_rows, out_grad, gate_weight, up_weight, down_weight, expert_ids, slot_expert):
    expert_here = lax.axis_index("expert")
    n_expert = lax.axis_size("expert")
    n_replica = lax.axis_size("replica")
    rows, features = x_rows.shape
    part = features // n_replica
    experts_all = EXP_DEV * n_expert
    capacity = max(2, 2 * rows // experts_all)
    slots = experts_all * capacity
    own_row = lax.dynamic_index_in_dim(slot_expert, expert_here, 0, keepdims=False)
    local_all = own_row - EXP_DEV * expert_here
    servers = jnp.sum(
        (jnp.arange(EXP_DEV, dtype=jnp.int32)[:, None] == local_all[None, :]).astype(F32), axis=1
    )[:, None, None]

    slot_row = send_slots(expert_ids, experts_all, capacity)
    slot_row = jnp.pad(slot_row.astype(BF), (0, part - rows))
    slot_rows = jnp.broadcast_to(slot_row[None, None, :], (n_replica, 16, part))
    split = lambda a: a.reshape(rows, n_replica, part).transpose(1, 0, 2)
    outgoing = jnp.concatenate([split(x_rows), split(out_grad), slot_rows], axis=1)
    arrived = lax.all_to_all(outgoing, "replica", split_axis=0, concat_axis=0, tiled=True)
    slot_of = arrived[:, 2 * rows, :rows].astype(jnp.int32)
    pick = (
        slot_of[:, None, :] == lax.broadcasted_iota(jnp.int32, (n_replica, slots, rows), 1)
    ).astype(BF)
    pairs = arrived[:, : 2 * rows].reshape(n_replica, 2, rows, part)
    packed = jnp.einsum("qsr,qarf->saqf", pick, pairs, preferred_element_type=F32).astype(BF)
    packed = packed.reshape(n_expert, EXP_DEV * capacity, 2, n_replica, part)
    packed = lax.all_to_all(packed, "expert", split_axis=0, concat_axis=0, tiled=True)
    packed = packed.reshape(n_expert, EXP_DEV, capacity, 2, n_replica, part)
    packed = packed.transpose(3, 1, 0, 4, 2, 5).reshape(2, EXP_DEV, -1, part)

    slot_grad, gate_sum, up_sum, down_sum = middle(
        n_replica, packed[0], packed[1], gate_weight, up_weight, down_weight
    )
    back = slot_grad.reshape(EXP_DEV, n_expert, n_replica, capacity, part).transpose(1, 2, 0, 3, 4)
    back = lax.all_to_all(back, "expert", split_axis=0, concat_axis=0, tiled=True)
    back = back.transpose(1, 0, 2, 3, 4).reshape(n_replica, slots, part)
    x_part = jnp.einsum("qsr,qsf->qrf", pick, back, preferred_element_type=F32).astype(BF)
    x_grad = lax.all_to_all(x_part, "replica", split_axis=0, concat_axis=0, tiled=True)
    x_grad = x_grad.transpose(1, 0, 2).reshape(rows, features)
    mean = lambda total: (total / servers).astype(BF)
    return (x_grad, mean(gate_sum), mean(up_sum), mean(down_sum))


def solution(mesh):
    return jax.shard_map(
        on_device,
        mesh=mesh,
        in_specs=(
            P(("expert", "replica"), None),
            P(("expert", "replica"), None),
            P("expert", "replica", None),
            P("expert", "replica", None),
            P("expert", "replica", None),
            P(("expert", "replica")),
            P(),
        ),
        out_specs=(
            P(("expert", "replica"), None),
            P("expert", "replica", None),
            P("expert", "replica", None),
            P("expert", "replica", None),
        ),
        check_vma=False,
    )
```

```python
import functools

import jax
import jax.numpy as jnp
from jax import lax
from jax.experimental import pallas as pl
from jax.experimental.pallas import tpu as pltpu
from jax.sharding import PartitionSpec as P

EXP_DEV = 2
BF = jnp.bfloat16
F32 = jnp.float32


def send_slots(row_experts, expert_count, capacity):
    rows = row_experts.shape[0]
    expert_range = lax.broadcasted_iota(jnp.int32, (rows, expert_count), 1)
    one_hot = (expert_range == row_experts[:, None]).astype(BF)
    earlier = lax.broadcasted_iota(jnp.int32, (rows, rows), 1) < lax.broadcasted_iota(
        jnp.int32, (rows, rows), 0
    )
    before = jnp.dot(earlier.astype(BF), one_hot, preferred_element_type=F32)
    rank = jnp.sum(before * one_hot.astype(F32), axis=1)
    return row_experts.astype(F32) * capacity + rank


HOP_STEPS = 2


def flip(index, other, size):
    result, bit = 0, 1
    while bit < size:
        result = result + lax.rem(index // bit + other // bit, 2) * bit
        bit *= 2
    return result


def line_kernel(
    n_expert, n_replica, packed, a_ref, b_ref, c_ref, pairs, ret, gate_ref, up_ref, hid_ref,
    own, from_left, from_right, to_right, to_left, back, total,
    send_r, recv_r, send_l, recv_l, send_p, recv_p, send_b, recv_b,
):
    here = lax.axis_index("replica")
    index = lax.axis_index("expert")
    last = n_replica - 1
    n_chunk, chunk, _ = own.shape
    hidden = a_ref.shape[2]
    rows = packed.shape[2]
    per_source = rows // chunk
    per_expert = rows // EXP_DEV
    mesh_id = pl.DeviceIdType.MESH

    def rightward(c):
        return pltpu.make_async_remote_copy(
            src_ref=to_right.at[c], dst_ref=from_left.at[c],
            send_sem=send_r.at[c], recv_sem=recv_r.at[c],
            device_id={"replica": lax.rem(here + 1, n_replica)}, device_id_type=mesh_id,
        )

    def leftward(c):
        return pltpu.make_async_remote_copy(
            src_ref=to_left.at[c], dst_ref=from_right.at[c],
            send_sem=send_l.at[c], recv_sem=recv_l.at[c],
            device_id={"replica": lax.rem(here + last, n_replica)}, device_id_type=mesh_id,
        )

    def outward(k):
        return pltpu.make_async_remote_copy(
            src_ref=packed.at[k], dst_ref=pairs.at[k],
            send_sem=send_p.at[k], recv_sem=recv_p.at[k],
            device_id={"expert": flip(index, k, n_expert)}, device_id_type=mesh_id,
        )

    def homeward(k):
        return pltpu.make_async_remote_copy(
            src_ref=back.at[k], dst_ref=ret.at[k],
            send_sem=send_b.at[k], recv_sem=recv_b.at[k],
            device_id={"expert": flip(index, k, n_expert)}, device_id_type=mesh_id,
        )

    barrier = pltpu.get_barrier_semaphore()

    @pl.loop(1, n_expert)
    def _(k):
        pl.semaphore_signal(
            barrier, inc=1, device_id={"expert": flip(index, k, n_expert)}, device_id_type=mesh_id
        )

    @pl.when(here > 0)
    def _():
        pl.semaphore_signal(
            barrier, inc=1, device_id={"replica": lax.rem(here + last, n_replica)},
            device_id_type=mesh_id,
        )

    @pl.when(here < last)
    def _():
        pl.semaphore_signal(
            barrier, inc=1, device_id={"replica": lax.rem(here + 1, n_replica)},
            device_id_type=mesh_id,
        )

    pairs[0] = packed[0]

    @pl.when((here > 0) & (here < last))
    def _():
        pl.semaphore_wait(barrier, n_expert + 1)

    @pl.when((here == 0) | (here == last))
    def _():
        pl.semaphore_wait(barrier, n_expert)

    @pl.loop(1, n_expert)
    def _(k):
        outward(k).start()

    def by_expert(product):
        if per_expert % 16 == 0:
            return jnp.concatenate(
                [product(slice(e * per_expert, (e + 1) * per_expert), e) for e in range(EXP_DEV)],
                axis=0,
            )
        both = [product(slice(0, rows), e) for e in range(EXP_DEV)]
        first = lax.broadcasted_iota(jnp.int32, both[0].shape, 0) < per_expert
        return jnp.where(first, both[0], both[1])

    def first_products(k):
        for w, (side, rhs) in enumerate(((0, a_ref), (0, b_ref), (1, c_ref))):
            part = by_expert(
                lambda at, e: jnp.dot(pairs[k, side, at, :], rhs[e], preferred_element_type=F32)
            )
            own[pl.ds(k * per_source, per_source), :, w * hidden : (w + 1) * hidden] = part.reshape(
                per_source, chunk, hidden
            )

    def slot_gradient(k):
        at_k = pl.ds(k * per_source, per_source)
        gate_part = gate_ref[at_k].reshape(rows, hidden)
        up_part = up_ref[at_k].reshape(rows, hidden)
        dims = (((1,), (1,)), ((), ()))
        return by_expert(
            lambda at, e: lax.dot_general(
                gate_part[at], a_ref[e], dims, preferred_element_type=F32
            )
            + lax.dot_general(up_part[at], b_ref[e], dims, preferred_element_type=F32)
        ).astype(BF)

    @pl.loop(0, n_chunk + HOP_STEPS * last)
    def _(t):
        c_left = t - HOP_STEPS * here
        c_right = t - HOP_STEPS * (last - here)
        done = t - HOP_STEPS * last

        @pl.when((t < n_chunk) & (lax.rem(t, per_source) == 0))
        def _():
            k = t // per_source

            @pl.when(k > 0)
            def _():
                outward(k).wait_recv()

            first_products(k)

        @pl.when((here == 0) & (t < n_chunk))
        def _():
            to_right[t] = own[t].astype(BF)
            rightward(t).start()

        @pl.when((here == last) & (t < n_chunk))
        def _():
            to_left[t] = own[t].astype(BF)
            leftward(t).start()

        @pl.when((here > 0) & (c_left >= 0) & (c_left < n_chunk))
        def _():
            rightward(c_left).wait_recv()

            @pl.when(here < last)
            def _():
                to_right[c_left] = (own[c_left] + from_left[c_left].astype(F32)).astype(BF)
                rightward(c_left).start()

        @pl.when((here < last) & (c_right >= 0) & (c_right < n_chunk))
        def _():
            leftward(c_right).wait_recv()

            @pl.when(here > 0)
            def _():
                to_left[c_right] = (own[c_right] + from_right[c_right].astype(F32)).astype(BF)
                leftward(c_right).start()

        @pl.when(done >= 0)
        def _():
            total[...] = own[done]

            @pl.when(here > 0)
            def _():
                total[...] += from_left[done].astype(F32)

            @pl.when(here < last)
            def _():
                total[...] += from_right[done].astype(F32)

            gate_pre = total[:, :hidden]
            up_pre = total[:, hidden : 2 * hidden]
            hidden_grad = total[:, 2 * hidden :]
            sig = jax.nn.sigmoid(gate_pre)
            silu = gate_pre * sig
            hid_ref[done] = (silu * up_pre).astype(BF)
            up_ref[done] = (hidden_grad * silu).astype(BF)
            gate_ref[done] = (
                hidden_grad * up_pre * sig * (1.0 + gate_pre * (1.0 - sig))
            ).astype(BF)

        @pl.when((done >= 0) & (lax.rem(t - HOP_STEPS * last + per_source, per_source) == per_source - 1))
        def _():
            k = done // per_source

            @pl.when(k == 0)
            def _():
                ret[0] = slot_gradient(0)

            @pl.when(k > 0)
            def _():
                back[k] = slot_gradient(k)
                homeward(k).start()

    @pl.loop(1, n_expert)
    def _(k):
        homeward(k).wait_recv()
        homeward(k).wait_send()
        outward(k).wait_send()

    @pl.loop(0, n_chunk)
    def _(c):
        @pl.when(here < last)
        def _():
            rightward(c).wait_send()

        @pl.when(here > 0)
        def _():
            leftward(c).wait_send()


def middle(n_expert, n_replica, packed, gate_w, up_w, down_w):
    rows, part = packed.shape[2:]
    hidden = gate_w.shape[2]
    chunk = min(32, rows)
    n_chunk = n_expert * rows // chunk
    wide = (n_chunk, chunk, 3 * hidden)
    vmem = pl.BlockSpec(memory_space=pltpu.VMEM)
    one_way = jax.ShapeDtypeStruct((n_expert, rows, part), BF)
    pairs, ret, gate_part, up_part, hid = pl.pallas_call(
        functools.partial(line_kernel, n_expert, n_replica),
        out_shape=[jax.ShapeDtypeStruct(packed.shape, BF), one_way]
        + [jax.ShapeDtypeStruct((n_chunk, chunk, hidden), BF)] * 3,
        in_specs=[vmem] * 4,
        out_specs=[vmem] * 5,
        scratch_shapes=[
            pltpu.VMEM(wide, F32),
            pltpu.VMEM(wide, BF),
            pltpu.VMEM(wide, BF),
            pltpu.VMEM(wide, BF),
            pltpu.VMEM(wide, BF),
            pltpu.VMEM(one_way.shape, BF),
            pltpu.VMEM(wide[1:], F32),
        ]
        + [pltpu.SemaphoreType.DMA((n_chunk,))] * 4
        + [pltpu.SemaphoreType.DMA((n_expert,))] * 4,
        compiler_params=pltpu.CompilerParams(
            collective_id=0, has_side_effects=True, vmem_limit_bytes=56 * 2**20
        ),
        cost_estimate=pl.CostEstimate(
            flops=10 * n_expert * rows * part * hidden,
            bytes_accessed=2**24,
            transcendentals=2**20,
        ),
    )(packed, gate_w, up_w, down_w)
    fold = lambda a: a.reshape(n_expert, EXP_DEV, rows // EXP_DEV, -1)
    term = lambda a, b: jnp.einsum(
        "kerf,kerh->efh", fold(a), fold(b), preferred_element_type=F32
    )
    rows_in, rows_grad = pairs[:, 0], pairs[:, 1]
    return (ret, term(rows_in, gate_part), term(rows_in, up_part), term(rows_grad, hid))


def on_device(x_rows, out_grad, gate_weight, up_weight, down_weight, expert_ids, slot_expert):
    expert_here = lax.axis_index("expert")
    n_expert = lax.axis_size("expert")
    n_replica = lax.axis_size("replica")
    rows, features = x_rows.shape
    part = features // n_replica
    experts_all = EXP_DEV * n_expert
    capacity = max(2, 2 * rows // experts_all)
    own_row = lax.dynamic_index_in_dim(slot_expert, expert_here, 0, keepdims=False)
    local_all = own_row - EXP_DEV * expert_here
    servers = jnp.sum(
        (jnp.arange(EXP_DEV, dtype=jnp.int32)[:, None] == local_all[None, :]).astype(F32), axis=1
    )[:, None, None]

    slot_row = send_slots(expert_ids, experts_all, capacity)
    slot_row = jnp.pad(slot_row.astype(BF), (0, part - rows))
    slot_rows = jnp.broadcast_to(slot_row[None, None, :], (n_replica, 16, part))
    split = lambda a: a.reshape(rows, n_replica, part).transpose(1, 0, 2)
    outgoing = jnp.concatenate([split(x_rows), split(out_grad), slot_rows], axis=1)
    arrived = lax.all_to_all(outgoing, "replica", split_axis=0, concat_axis=0, tiled=True)
    slot_of = arrived[:, 2 * rows, :rows].astype(jnp.int32)
    source = jnp.bitwise_xor(expert_here, jnp.arange(n_expert, dtype=jnp.int32))
    group = EXP_DEV * capacity
    place = (source[:, None] * group + jnp.arange(group, dtype=jnp.int32)[None, :]).reshape(-1)
    pick = (slot_of[:, None, :] == place[None, :, None]).astype(BF)
    pick = pick.reshape(n_replica, n_expert, EXP_DEV, capacity, rows)
    pairs = arrived[:, : 2 * rows].reshape(n_replica, 2, rows, part)
    packed = jnp.einsum("qkecr,qarf->kaeqcf", pick, pairs, preferred_element_type=F32).astype(BF)
    packed = packed.reshape(n_expert, 2, n_replica * group, part)
    back, gate_sum, up_sum, down_sum = middle(
        n_expert, n_replica, packed, gate_weight, up_weight, down_weight
    )
    back = back.reshape(n_expert, EXP_DEV, n_replica, capacity, part)
    x_part = jnp.einsum("qkecr,keqcf->qrf", pick, back, preferred_element_type=F32).astype(BF)
    x_grad = lax.all_to_all(x_part, "replica", split_axis=0, concat_axis=0, tiled=True)
    x_grad = x_grad.transpose(1, 0, 2).reshape(rows, features)
    mean = lambda total: (total / servers).astype(BF)
    return (x_grad, mean(gate_sum), mean(up_sum), mean(down_sum))


def solution(mesh):
    return jax.shard_map(
        on_device,
        mesh=mesh,
        in_specs=(
            P(("expert", "replica"), None),
            P(("expert", "replica"), None),
            P("expert", "replica", None),
            P("expert", "replica", None),
            P("expert", "replica", None),
            P(("expert", "replica")),
            P(),
        ),
        out_specs=(
            P(("expert", "replica"), None),
            P("expert", "replica", None),
            P("expert", "replica", None),
            P("expert", "replica", None),
        ),
        check_vma=False,
    )
```

```python
import functools

import jax
import jax.numpy as jnp
from jax import lax
from jax.experimental import pallas as pl
from jax.experimental.pallas import tpu as pltpu
from jax.sharding import PartitionSpec as P

EXP_DEV = 2
BF = jnp.bfloat16
F32 = jnp.float32


def send_slots(row_experts, expert_count, capacity):
    rows = row_experts.shape[0]
    expert_range = lax.broadcasted_iota(jnp.int32, (rows, expert_count), 1)
    one_hot = (expert_range == row_experts[:, None]).astype(BF)
    earlier = lax.broadcasted_iota(jnp.int32, (rows, rows), 1) < lax.broadcasted_iota(
        jnp.int32, (rows, rows), 0
    )
    before = jnp.dot(earlier.astype(BF), one_hot, preferred_element_type=F32)
    rank = jnp.sum(before * one_hot.astype(F32), axis=1)
    return row_experts.astype(F32) * capacity + rank


HOP_STEPS = 2


def flip(index, other, size):
    result, bit = 0, 1
    while bit < size:
        result = result + lax.rem(index // bit + other // bit, 2) * bit
        bit *= 2
    return result


def line_kernel(
    n_expert, n_replica, x_ref, g_ref, slot_ref, a_ref, b_ref, c_ref,
    pairs, ret, gate_ref, up_ref, hid_ref, slots_in,
    x_in, g_in, packed, own, from_left, from_right, to_right, to_left, back, total,
    send_r, recv_r, send_l, recv_l, send_p, recv_p, send_b, recv_b, send_z, recv_z,
):
    here = lax.axis_index("replica")
    index = lax.axis_index("expert")
    last = n_replica - 1
    n_chunk, chunk, _ = own.shape
    hidden = a_ref.shape[2]
    rows = pairs.shape[2]
    per_source = rows // chunk
    per_expert = rows // EXP_DEV
    held = x_ref.shape[0]
    part = x_in.shape[1]
    group = rows // n_replica
    capacity = group // EXP_DEV
    mesh_id = pl.DeviceIdType.MESH

    def rightward(c):
        return pltpu.make_async_remote_copy(
            src_ref=to_right.at[c], dst_ref=from_left.at[c],
            send_sem=send_r.at[c], recv_sem=recv_r.at[c],
            device_id={"replica": lax.rem(here + 1, n_replica)}, device_id_type=mesh_id,
        )

    def leftward(c):
        return pltpu.make_async_remote_copy(
            src_ref=to_left.at[c], dst_ref=from_right.at[c],
            send_sem=send_l.at[c], recv_sem=recv_l.at[c],
            device_id={"replica": lax.rem(here + last, n_replica)}, device_id_type=mesh_id,
        )

    def outward(k):
        return pltpu.make_async_remote_copy(
            src_ref=packed.at[k], dst_ref=pairs.at[k],
            send_sem=send_p.at[k], recv_sem=recv_p.at[k],
            device_id={"expert": flip(index, k, n_expert)}, device_id_type=mesh_id,
        )

    def homeward(k):
        return pltpu.make_async_remote_copy(
            src_ref=back.at[k], dst_ref=ret.at[k],
            send_sem=send_b.at[k], recv_sem=recv_b.at[k],
            device_id={"expert": flip(index, k, n_expert)}, device_id_type=mesh_id,
        )

    def quarters(q):
        columns = pl.ds(pl.multiple_of(q * part, part), part)
        at = pl.ds(pl.multiple_of(here * held, held), held)
        return (
            (x_ref.at[:, columns], x_in.at[at]),
            (g_ref.at[:, columns], g_in.at[at]),
            (slot_ref, slots_in.at[here]),
        )

    def across(q):
        return [
            pltpu.make_async_remote_copy(
                src_ref=src, dst_ref=dst, send_sem=send_z.at[w, q], recv_sem=recv_z.at[w, here],
                device_id={"replica": q}, device_id_type=mesh_id,
            )
            for w, (src, dst) in enumerate(quarters(q))
        ]

    def arriving(q):
        at = pl.ds(pl.multiple_of(q * held, held), held)
        landed = (x_in.at[at], g_in.at[at], slots_in.at[q])
        return [
            pltpu.make_async_remote_copy(
                src_ref=dst, dst_ref=dst, send_sem=send_z.at[w, q], recv_sem=recv_z.at[w, q],
                device_id={"replica": q}, device_id_type=mesh_id,
            )
            for w, dst in enumerate(landed)
        ]

    barrier = pltpu.get_barrier_semaphore()

    @pl.loop(1, n_expert)
    def _(k):
        pl.semaphore_signal(
            barrier, inc=1, device_id={"expert": flip(index, k, n_expert)}, device_id_type=mesh_id
        )

    @pl.loop(1, n_replica)
    def _(k):
        pl.semaphore_signal(
            barrier, inc=1, device_id={"replica": lax.rem(here + k, n_replica)},
            device_id_type=mesh_id,
        )

    pl.semaphore_wait(barrier, n_expert + n_replica - 2)

    @pl.loop(1, n_replica)
    def _(k):
        for copy in across(lax.rem(here + k, n_replica)):
            copy.start()

    mine = [
        pltpu.make_async_copy(src, dst, send_z.at[w, here])
        for w, (src, dst) in enumerate(quarters(here))
    ]
    for copy in mine:
        copy.start()
    for copy in mine:
        copy.wait()

    @pl.loop(1, n_replica)
    def _(k):
        for copy in arriving(lax.rem(here + k, n_replica)):
            copy.wait_recv()

    span = n_expert * group
    keys = jnp.concatenate(
        [slots_in[q, 0:1, :].astype(F32) + float(q * span) for q in range(n_replica)], axis=1
    ).astype(jnp.int32)

    def pack(k):
        row = lax.broadcasted_iota(jnp.int32, (rows, 1), 0)
        local = row // per_expert
        sender = (row // capacity) % n_replica
        want = (
            sender * span
            + flip(index, k, n_expert) * group
            + local * capacity
            + row % capacity
        )
        pick = jnp.where(want == keys, 1.0, 0.0).astype(BF)
        return [
            jnp.dot(pick, side[...], preferred_element_type=F32).astype(BF)
            for side in (x_in, g_in)
        ]

    pairs[0, 0], pairs[0, 1] = pack(0)

    @pl.loop(1, n_expert)
    def _(k):
        packed[k, 0], packed[k, 1] = pack(k)
        outward(k).start()

    def by_expert(product):
        if per_expert % 16 == 0:
            return jnp.concatenate(
                [product(slice(e * per_expert, (e + 1) * per_expert), e) for e in range(EXP_DEV)],
                axis=0,
            )
        both = [product(slice(0, rows), e) for e in range(EXP_DEV)]
        first = lax.broadcasted_iota(jnp.int32, both[0].shape, 0) < per_expert
        return jnp.where(first, both[0], both[1])

    def first_products(k):
        for w, (side, rhs) in enumerate(((0, a_ref), (0, b_ref), (1, c_ref))):
            part = by_expert(
                lambda at, e: jnp.dot(pairs[k, side, at, :], rhs[e], preferred_element_type=F32)
            )
            own[pl.ds(k * per_source, per_source), :, w * hidden : (w + 1) * hidden] = part.reshape(
                per_source, chunk, hidden
            )

    def slot_gradient(k):
        at_k = pl.ds(k * per_source, per_source)
        gate_part = gate_ref[at_k].reshape(rows, hidden)
        up_part = up_ref[at_k].reshape(rows, hidden)
        dims = (((1,), (1,)), ((), ()))
        return by_expert(
            lambda at, e: lax.dot_general(
                gate_part[at], a_ref[e], dims, preferred_element_type=F32
            )
            + lax.dot_general(up_part[at], b_ref[e], dims, preferred_element_type=F32)
        ).astype(BF)

    @pl.loop(0, n_chunk + HOP_STEPS * last)
    def _(t):
        c_left = t - HOP_STEPS * here
        c_right = t - HOP_STEPS * (last - here)
        done = t - HOP_STEPS * last

        @pl.when((t < n_chunk) & (lax.rem(t, per_source) == 0))
        def _():
            k = t // per_source

            @pl.when(k > 0)
            def _():
                outward(k).wait_recv()

            first_products(k)

        @pl.when((here == 0) & (t < n_chunk))
        def _():
            to_right[t] = own[t].astype(BF)
            rightward(t).start()

        @pl.when((here == last) & (t < n_chunk))
        def _():
            to_left[t] = own[t].astype(BF)
            leftward(t).start()

        @pl.when((here > 0) & (c_left >= 0) & (c_left < n_chunk))
        def _():
            rightward(c_left).wait_recv()

            @pl.when(here < last)
            def _():
                to_right[c_left] = (own[c_left] + from_left[c_left].astype(F32)).astype(BF)
                rightward(c_left).start()

        @pl.when((here < last) & (c_right >= 0) & (c_right < n_chunk))
        def _():
            leftward(c_right).wait_recv()

            @pl.when(here > 0)
            def _():
                to_left[c_right] = (own[c_right] + from_right[c_right].astype(F32)).astype(BF)
                leftward(c_right).start()

        @pl.when(done >= 0)
        def _():
            total[...] = own[done]

            @pl.when(here > 0)
            def _():
                total[...] += from_left[done].astype(F32)

            @pl.when(here < last)
            def _():
                total[...] += from_right[done].astype(F32)

            gate_pre = total[:, :hidden]
            up_pre = total[:, hidden : 2 * hidden]
            hidden_grad = total[:, 2 * hidden :]
            sig = jax.nn.sigmoid(gate_pre)
            silu = gate_pre * sig
            hid_ref[done] = (silu * up_pre).astype(BF)
            up_ref[done] = (hidden_grad * silu).astype(BF)
            gate_ref[done] = (
                hidden_grad * up_pre * sig * (1.0 + gate_pre * (1.0 - sig))
            ).astype(BF)

        @pl.when((done >= 0) & (lax.rem(t - HOP_STEPS * last + per_source, per_source) == per_source - 1))
        def _():
            k = done // per_source

            @pl.when(k == 0)
            def _():
                ret[0] = slot_gradient(0)

            @pl.when(k > 0)
            def _():
                back[k] = slot_gradient(k)
                homeward(k).start()

    @pl.loop(1, n_expert)
    def _(k):
        homeward(k).wait_recv()
        homeward(k).wait_send()
        outward(k).wait_send()

    @pl.loop(1, n_replica)
    def _(k):
        for copy in across(lax.rem(here + k, n_replica)):
            copy.wait_send()

    @pl.loop(0, n_chunk)
    def _(c):
        @pl.when(here < last)
        def _():
            rightward(c).wait_send()

        @pl.when(here > 0)
        def _():
            leftward(c).wait_send()


def middle(n_expert, n_replica, capacity, x_rows, out_grad, slot_rows, gate_w, up_w, down_w):
    rows, part = EXP_DEV * n_replica * capacity, gate_w.shape[1]
    held = x_rows.shape[0]
    both = (n_expert, 2, rows, part)
    hidden = gate_w.shape[2]
    chunk = min(32, rows)
    n_chunk = n_expert * rows // chunk
    wide = (n_chunk, chunk, 3 * hidden)
    vmem = pl.BlockSpec(memory_space=pltpu.VMEM)
    one_way = jax.ShapeDtypeStruct((n_expert, rows, part), BF)
    pairs, ret, gate_part, up_part, hid, slots_in = pl.pallas_call(
        functools.partial(line_kernel, n_expert, n_replica),
        out_shape=[jax.ShapeDtypeStruct(both, BF), one_way]
        + [jax.ShapeDtypeStruct((n_chunk, chunk, hidden), BF)] * 3
        + [jax.ShapeDtypeStruct((n_replica,) + slot_rows.shape, BF)],
        in_specs=[vmem] * 6,
        out_specs=[vmem] * 6,
        scratch_shapes=[
            pltpu.VMEM((n_replica * held, part), BF),
            pltpu.VMEM((n_replica * held, part), BF),
            pltpu.VMEM(both, BF),
            pltpu.VMEM(wide, F32),
            pltpu.VMEM(wide, BF),
            pltpu.VMEM(wide, BF),
            pltpu.VMEM(wide, BF),
            pltpu.VMEM(wide, BF),
            pltpu.VMEM(one_way.shape, BF),
            pltpu.VMEM(wide[1:], F32),
        ]
        + [pltpu.SemaphoreType.DMA((n_chunk,))] * 4
        + [pltpu.SemaphoreType.DMA((n_expert,))] * 4
        + [pltpu.SemaphoreType.DMA((3, n_replica))] * 2,
        compiler_params=pltpu.CompilerParams(
            collective_id=0, has_side_effects=True, vmem_limit_bytes=56 * 2**20
        ),
        cost_estimate=pl.CostEstimate(
            flops=10 * n_expert * rows * part * hidden,
            bytes_accessed=2**24,
            transcendentals=2**20,
        ),
    )(x_rows, out_grad, slot_rows, gate_w, up_w, down_w)
    fold = lambda a: a.reshape(n_expert, EXP_DEV, rows // EXP_DEV, -1)
    term = lambda a, b: jnp.einsum(
        "kerf,kerh->efh", fold(a), fold(b), preferred_element_type=F32
    )
    rows_in, rows_grad = pairs[:, 0], pairs[:, 1]
    return (ret, slots_in, term(rows_in, gate_part), term(rows_in, up_part), term(rows_grad, hid))


def on_device(x_rows, out_grad, gate_weight, up_weight, down_weight, expert_ids, slot_expert):
    expert_here = lax.axis_index("expert")
    n_expert = lax.axis_size("expert")
    n_replica = lax.axis_size("replica")
    rows, features = x_rows.shape
    part = features // n_replica
    experts_all = EXP_DEV * n_expert
    capacity = max(2, 2 * rows // experts_all)
    own_row = lax.dynamic_index_in_dim(slot_expert, expert_here, 0, keepdims=False)
    local_all = own_row - EXP_DEV * expert_here
    servers = jnp.sum(
        (jnp.arange(EXP_DEV, dtype=jnp.int32)[:, None] == local_all[None, :]).astype(F32), axis=1
    )[:, None, None]

    slot_row = send_slots(expert_ids, experts_all, capacity)
    slot_rows = jnp.broadcast_to(slot_row.astype(BF)[None, :], (16, rows))
    back, slots_in, gate_sum, up_sum, down_sum = middle(
        n_expert, n_replica, capacity, x_rows, out_grad, slot_rows,
        gate_weight, up_weight, down_weight,
    )
    slot_of = slots_in[:, 0, :].astype(jnp.int32)
    source = jnp.bitwise_xor(expert_here, jnp.arange(n_expert, dtype=jnp.int32))
    group = EXP_DEV * capacity
    place = (source[:, None] * group + jnp.arange(group, dtype=jnp.int32)[None, :]).reshape(-1)
    pick = (slot_of[:, None, :] == place[None, :, None]).astype(BF)
    pick = pick.reshape(n_replica, n_expert, EXP_DEV, capacity, rows)
    back = back.reshape(n_expert, EXP_DEV, n_replica, capacity, part)
    x_part = jnp.einsum("qkecr,keqcf->qrf", pick, back, preferred_element_type=F32).astype(BF)
    x_grad = lax.all_to_all(x_part, "replica", split_axis=0, concat_axis=0, tiled=True)
    x_grad = x_grad.transpose(1, 0, 2).reshape(rows, features)
    mean = lambda total: (total / servers).astype(BF)
    return (x_grad, mean(gate_sum), mean(up_sum), mean(down_sum))


def solution(mesh):
    return jax.shard_map(
        on_device,
        mesh=mesh,
        in_specs=(
            P(("expert", "replica"), None),
            P(("expert", "replica"), None),
            P("expert", "replica", None),
            P("expert", "replica", None),
            P("expert", "replica", None),
            P(("expert", "replica")),
            P(),
        ),
        out_specs=(
            P(("expert", "replica"), None),
            P("expert", "replica", None),
            P("expert", "replica", None),
            P("expert", "replica", None),
        ),
        check_vma=False,
    )
```

```python
import functools

import jax
import jax.numpy as jnp
from jax import lax
from jax.experimental import pallas as pl
from jax.experimental.pallas import tpu as pltpu
from jax.sharding import PartitionSpec as P

EXP_DEV = 2
BF = jnp.bfloat16
F32 = jnp.float32


def send_slots(row_experts, expert_count, capacity):
    rows = row_experts.shape[0]
    expert_range = lax.broadcasted_iota(jnp.int32, (rows, expert_count), 1)
    one_hot = (expert_range == row_experts[:, None]).astype(BF)
    earlier = lax.broadcasted_iota(jnp.int32, (rows, rows), 1) < lax.broadcasted_iota(
        jnp.int32, (rows, rows), 0
    )
    before = jnp.dot(earlier.astype(BF), one_hot, preferred_element_type=F32)
    rank = jnp.sum(before * one_hot.astype(F32), axis=1)
    return row_experts.astype(F32) * capacity + rank


HOP_STEPS = 2


def flip(index, other, size):
    result, bit = 0, 1
    while bit < size:
        result = result + lax.rem(index // bit + other // bit, 2) * bit
        bit *= 2
    return result


def line_kernel(
    n_expert, n_replica, x_ref, g_ref, slot_ref, a_ref, b_ref, c_ref,
    pairs, ret, gate_ref, up_ref, hid_ref, slots_in,
    x_in, g_in, packed, own, from_left, from_right, to_right, to_left, back, total,
    send_r, recv_r, send_l, recv_l, send_p, recv_p, send_b, recv_b, send_z, recv_z,
):
    here = lax.axis_index("replica")
    index = lax.axis_index("expert")
    last = n_replica - 1
    n_chunk, chunk, _ = own.shape
    hidden = a_ref.shape[2]
    rows = pairs.shape[2]
    per_source = rows // chunk
    per_expert = rows // EXP_DEV
    held = x_ref.shape[0]
    part = x_in.shape[1]
    group = rows // n_replica
    capacity = group // EXP_DEV
    mesh_id = pl.DeviceIdType.MESH

    def rightward(c):
        return pltpu.make_async_remote_copy(
            src_ref=to_right.at[c], dst_ref=from_left.at[c],
            send_sem=send_r.at[c], recv_sem=recv_r.at[c],
            device_id={"replica": lax.rem(here + 1, n_replica)}, device_id_type=mesh_id,
        )

    def leftward(c):
        return pltpu.make_async_remote_copy(
            src_ref=to_left.at[c], dst_ref=from_right.at[c],
            send_sem=send_l.at[c], recv_sem=recv_l.at[c],
            device_id={"replica": lax.rem(here + last, n_replica)}, device_id_type=mesh_id,
        )

    def outward(k):
        return pltpu.make_async_remote_copy(
            src_ref=packed.at[k], dst_ref=pairs.at[k],
            send_sem=send_p.at[k], recv_sem=recv_p.at[k],
            device_id={"expert": flip(index, k, n_expert)}, device_id_type=mesh_id,
        )

    def homeward(k):
        return pltpu.make_async_remote_copy(
            src_ref=back.at[k], dst_ref=ret.at[k],
            send_sem=send_b.at[k], recv_sem=recv_b.at[k],
            device_id={"expert": flip(index, k, n_expert)}, device_id_type=mesh_id,
        )

    def quarters(q):
        columns = pl.ds(pl.multiple_of(q * part, part), part)
        at = pl.ds(pl.multiple_of(here * held, held), held)
        return (
            (x_ref.at[:, columns], x_in.at[at]),
            (g_ref.at[:, columns], g_in.at[at]),
            (slot_ref, slots_in.at[here]),
        )

    def across(q):
        return [
            pltpu.make_async_remote_copy(
                src_ref=src, dst_ref=dst, send_sem=send_z.at[w, q], recv_sem=recv_z.at[w, here],
                device_id={"replica": q}, device_id_type=mesh_id,
            )
            for w, (src, dst) in enumerate(quarters(q))
        ]

    def arriving(q):
        at = pl.ds(pl.multiple_of(q * held, held), held)
        landed = (x_in.at[at], g_in.at[at], slots_in.at[q])
        return [
            pltpu.make_async_remote_copy(
                src_ref=dst, dst_ref=dst, send_sem=send_z.at[w, q], recv_sem=recv_z.at[w, q],
                device_id={"replica": q}, device_id_type=mesh_id,
            )
            for w, dst in enumerate(landed)
        ]

    barrier = pltpu.get_barrier_semaphore()

    @pl.loop(1, n_expert)
    def _(k):
        pl.semaphore_signal(
            barrier, inc=1, device_id={"expert": flip(index, k, n_expert)}, device_id_type=mesh_id
        )

    @pl.loop(1, n_replica)
    def _(k):
        pl.semaphore_signal(
            barrier, inc=1, device_id={"replica": lax.rem(here + k, n_replica)},
            device_id_type=mesh_id,
        )

    pl.semaphore_wait(barrier, n_expert + n_replica - 2)

    @pl.loop(1, n_replica)
    def _(k):
        for copy in across(lax.rem(here + k, n_replica)):
            copy.start()

    mine = [
        pltpu.make_async_copy(src, dst, send_z.at[w, here])
        for w, (src, dst) in enumerate(quarters(here))
    ]
    for copy in mine:
        copy.start()
    for copy in mine:
        copy.wait()

    @pl.loop(1, n_replica)
    def _(k):
        for copy in arriving(lax.rem(here + k, n_replica)):
            copy.wait_recv()

    span = n_expert * group
    keys = jnp.concatenate(
        [slots_in[q, 0:1, :].astype(F32) + float(q * span) for q in range(n_replica)], axis=1
    ).astype(jnp.int32)

    def pack(k):
        row = lax.broadcasted_iota(jnp.int32, (rows, 1), 0)
        local = row // per_expert
        sender = (row // capacity) % n_replica
        want = (
            sender * span
            + flip(index, k, n_expert) * group
            + local * capacity
            + row % capacity
        )
        pick = jnp.where(want == keys, 1.0, 0.0).astype(BF)
        return [
            jnp.dot(pick, side[...], preferred_element_type=F32).astype(BF)
            for side in (x_in, g_in)
        ]

    pairs[0, 0], pairs[0, 1] = pack(0)

    def by_expert(product):
        if per_expert % 16 == 0:
            return jnp.concatenate(
                [product(slice(e * per_expert, (e + 1) * per_expert), e) for e in range(EXP_DEV)],
                axis=0,
            )
        both = [product(slice(0, rows), e) for e in range(EXP_DEV)]
        first = lax.broadcasted_iota(jnp.int32, both[0].shape, 0) < per_expert
        return jnp.where(first, both[0], both[1])

    def first_products(k):
        for w, (side, rhs) in enumerate(((0, a_ref), (0, b_ref), (1, c_ref))):
            part = by_expert(
                lambda at, e: jnp.dot(pairs[k, side, at, :], rhs[e], preferred_element_type=F32)
            )
            own[pl.ds(k * per_source, per_source), :, w * hidden : (w + 1) * hidden] = part.reshape(
                per_source, chunk, hidden
            )

    def slot_gradient(k):
        at_k = pl.ds(k * per_source, per_source)
        gate_part = gate_ref[at_k].reshape(rows, hidden)
        up_part = up_ref[at_k].reshape(rows, hidden)
        dims = (((1,), (1,)), ((), ()))
        return by_expert(
            lambda at, e: lax.dot_general(
                gate_part[at], a_ref[e], dims, preferred_element_type=F32
            )
            + lax.dot_general(up_part[at], b_ref[e], dims, preferred_element_type=F32)
        ).astype(BF)

    @pl.loop(0, n_chunk + HOP_STEPS * last)
    def _(t):
        c_left = t - HOP_STEPS * here
        c_right = t - HOP_STEPS * (last - here)
        done = t - HOP_STEPS * last

        @pl.when((t < n_chunk) & (lax.rem(t, per_source) == 0))
        def _():
            k = t // per_source

            @pl.when(k > 0)
            def _():
                outward(k).wait_recv()

            first_products(k)

        @pl.when((here == 0) & (t < n_chunk))
        def _():
            to_right[t] = own[t].astype(BF)
            rightward(t).start()

        @pl.when((here == last) & (t < n_chunk))
        def _():
            to_left[t] = own[t].astype(BF)
            leftward(t).start()

        @pl.when(t < n_expert - 1)
        def _():
            k = t + 1
            packed[k, 0], packed[k, 1] = pack(k)
            outward(k).start()

        @pl.when((here > 0) & (c_left >= 0) & (c_left < n_chunk))
        def _():
            rightward(c_left).wait_recv()

            @pl.when(here < last)
            def _():
                to_right[c_left] = (own[c_left] + from_left[c_left].astype(F32)).astype(BF)
                rightward(c_left).start()

        @pl.when((here < last) & (c_right >= 0) & (c_right < n_chunk))
        def _():
            leftward(c_right).wait_recv()

            @pl.when(here > 0)
            def _():
                to_left[c_right] = (own[c_right] + from_right[c_right].astype(F32)).astype(BF)
                leftward(c_right).start()

        @pl.when(done >= 0)
        def _():
            total[...] = own[done]

            @pl.when(here > 0)
            def _():
                total[...] += from_left[done].astype(F32)

            @pl.when(here < last)
            def _():
                total[...] += from_right[done].astype(F32)

            gate_pre = total[:, :hidden]
            up_pre = total[:, hidden : 2 * hidden]
            hidden_grad = total[:, 2 * hidden :]
            sig = jax.nn.sigmoid(gate_pre)
            silu = gate_pre * sig
            hid_ref[done] = (silu * up_pre).astype(BF)
            up_ref[done] = (hidden_grad * silu).astype(BF)
            gate_ref[done] = (
                hidden_grad * up_pre * sig * (1.0 + gate_pre * (1.0 - sig))
            ).astype(BF)

        @pl.when((done >= 0) & (lax.rem(t - HOP_STEPS * last + per_source, per_source) == per_source - 1))
        def _():
            k = done // per_source

            @pl.when(k == 0)
            def _():
                ret[0] = slot_gradient(0)

            @pl.when(k > 0)
            def _():
                back[k] = slot_gradient(k)
                homeward(k).start()

    @pl.loop(1, n_expert)
    def _(k):
        homeward(k).wait_recv()
        homeward(k).wait_send()
        outward(k).wait_send()

    @pl.loop(1, n_replica)
    def _(k):
        for copy in across(lax.rem(here + k, n_replica)):
            copy.wait_send()

    @pl.loop(0, n_chunk)
    def _(c):
        @pl.when(here < last)
        def _():
            rightward(c).wait_send()

        @pl.when(here > 0)
        def _():
            leftward(c).wait_send()


def middle(n_expert, n_replica, capacity, x_rows, out_grad, slot_rows, gate_w, up_w, down_w):
    rows, part = EXP_DEV * n_replica * capacity, gate_w.shape[1]
    held = x_rows.shape[0]
    both = (n_expert, 2, rows, part)
    hidden = gate_w.shape[2]
    chunk = min(32, rows)
    n_chunk = n_expert * rows // chunk
    wide = (n_chunk, chunk, 3 * hidden)
    vmem = pl.BlockSpec(memory_space=pltpu.VMEM)
    one_way = jax.ShapeDtypeStruct((n_expert, rows, part), BF)
    pairs, ret, gate_part, up_part, hid, slots_in = pl.pallas_call(
        functools.partial(line_kernel, n_expert, n_replica),
        out_shape=[jax.ShapeDtypeStruct(both, BF), one_way]
        + [jax.ShapeDtypeStruct((n_chunk, chunk, hidden), BF)] * 3
        + [jax.ShapeDtypeStruct((n_replica,) + slot_rows.shape, BF)],
        in_specs=[vmem] * 6,
        out_specs=[vmem] * 6,
        scratch_shapes=[
            pltpu.VMEM((n_replica * held, part), BF),
            pltpu.VMEM((n_replica * held, part), BF),
            pltpu.VMEM(both, BF),
            pltpu.VMEM(wide, F32),
            pltpu.VMEM(wide, BF),
            pltpu.VMEM(wide, BF),
            pltpu.VMEM(wide, BF),
            pltpu.VMEM(wide, BF),
            pltpu.VMEM(one_way.shape, BF),
            pltpu.VMEM(wide[1:], F32),
        ]
        + [pltpu.SemaphoreType.DMA((n_chunk,))] * 4
        + [pltpu.SemaphoreType.DMA((n_expert,))] * 4
        + [pltpu.SemaphoreType.DMA((3, n_replica))] * 2,
        compiler_params=pltpu.CompilerParams(
            collective_id=0, has_side_effects=True, vmem_limit_bytes=56 * 2**20
        ),
        cost_estimate=pl.CostEstimate(
            flops=10 * n_expert * rows * part * hidden,
            bytes_accessed=2**24,
            transcendentals=2**20,
        ),
    )(x_rows, out_grad, slot_rows, gate_w, up_w, down_w)
    fold = lambda a: a.reshape(n_expert, EXP_DEV, rows // EXP_DEV, -1)
    term = lambda a, b: jnp.einsum(
        "kerf,kerh->efh", fold(a), fold(b), preferred_element_type=F32
    )
    rows_in, rows_grad = pairs[:, 0], pairs[:, 1]
    return (ret, slots_in, term(rows_in, gate_part), term(rows_in, up_part), term(rows_grad, hid))


def on_device(x_rows, out_grad, gate_weight, up_weight, down_weight, expert_ids, slot_expert):
    expert_here = lax.axis_index("expert")
    n_expert = lax.axis_size("expert")
    n_replica = lax.axis_size("replica")
    rows, features = x_rows.shape
    part = features // n_replica
    experts_all = EXP_DEV * n_expert
    capacity = max(2, 2 * rows // experts_all)
    own_row = lax.dynamic_index_in_dim(slot_expert, expert_here, 0, keepdims=False)
    local_all = own_row - EXP_DEV * expert_here
    servers = jnp.sum(
        (jnp.arange(EXP_DEV, dtype=jnp.int32)[:, None] == local_all[None, :]).astype(F32), axis=1
    )[:, None, None]

    slot_row = send_slots(expert_ids, experts_all, capacity)
    slot_rows = jnp.broadcast_to(slot_row.astype(BF)[None, :], (16, rows))
    back, slots_in, gate_sum, up_sum, down_sum = middle(
        n_expert, n_replica, capacity, x_rows, out_grad, slot_rows,
        gate_weight, up_weight, down_weight,
    )
    slot_of = slots_in[:, 0, :].astype(jnp.int32)
    source = jnp.bitwise_xor(expert_here, jnp.arange(n_expert, dtype=jnp.int32))
    group = EXP_DEV * capacity
    place = (source[:, None] * group + jnp.arange(group, dtype=jnp.int32)[None, :]).reshape(-1)
    pick = (slot_of[:, None, :] == place[None, :, None]).astype(BF)
    pick = pick.reshape(n_replica, n_expert, EXP_DEV, capacity, rows)
    back = back.reshape(n_expert, EXP_DEV, n_replica, capacity, part)
    x_part = jnp.einsum("qkecr,keqcf->qrf", pick, back, preferred_element_type=F32).astype(BF)
    x_grad = lax.all_to_all(x_part, "replica", split_axis=0, concat_axis=0, tiled=True)
    x_grad = x_grad.transpose(1, 0, 2).reshape(rows, features)
    mean = lambda total: (total / servers).astype(BF)
    return (x_grad, mean(gate_sum), mean(up_sum), mean(down_sum))


def solution(mesh):
    return jax.shard_map(
        on_device,
        mesh=mesh,
        in_specs=(
            P(("expert", "replica"), None),
            P(("expert", "replica"), None),
            P("expert", "replica", None),
            P("expert", "replica", None),
            P("expert", "replica", None),
            P(("expert", "replica")),
            P(),
        ),
        out_specs=(
            P(("expert", "replica"), None),
            P("expert", "replica", None),
            P("expert", "replica", None),
            P("expert", "replica", None),
        ),
        check_vma=False,
    )
```
